128 devices in a mesh: vocab: 32 (over z, y, core), batch: 4 (over x).
Axes of the slice: x: 4, y: 4, z: 4, core: 2. Of those that a mesh axis runs over, the one named last changes fastest.
Arguments:
- hidden: bfloat16 [6144, 7168], P(('batch', 'vocab')), parts along dimension 0
- head_codes: bfloat16 [131072, 7168], P(('batch', 'vocab')), parts along dimension 0, may hold values from -4 to 4
- head_scales: float32 [1024, 56], P(('batch', 'vocab')), parts along dimension 0, may hold values from 0.01 to 0.1
Outputs:
- probabilities: bfloat16 [6144, 32768], P(('batch', 'vocab')), parts along dimension 0
- entropy: float32 [6144], P(('batch', 'vocab')), parts along dimension 0
The draws below stay inside these ranges and needn't reach their ends.
There are 4 independent parts, one for each index of `batch`. The reference program is written for one: setup_inputs(seed, part) draws one part's arguments, and reference() takes and returns one part's arrays. A program takes and returns all parts, laid end to end along the dimension named above; each array names one. Nothing has to cross between parts.
All inputs are finite; a program needn't handle non-finite values.
Results may differ from the reference program's by a relative error of at most 0.0098.
Values may be sent and summed in bfloat16 or wider, within the bound.
A program may use at most 192 MiB of HBM per device.

```python
import math
from functools import partial
import jax
import jax.numpy as jnp
from jax import lax

D = 7168
QBLOCK = 128
V_DEV = 1024
VOCAB = 32768
TOKENS = 1536
N_VOCAB = 32


def code_row(base_key, row_id):
    row_key = jax.random.fold_in(jax.random.fold_in(base_key, 7001), row_id)
    return jnp.clip(jax.random.normal(row_key, (D,), jnp.float32), -4.0, 4.0)


def scale_row(base_key, block_id):
    row_key = jax.random.fold_in(jax.random.fold_in(base_key, 7002), block_id)
    return jnp.exp(jax.random.uniform(row_key, (D // QBLOCK,), jnp.float32, math.log(0.01), math.log(0.1)))


def head_row(base_key, row_id):
    codes_row = code_row(base_key, row_id).astype(jnp.bfloat16).astype(jnp.float32)
    scales_row = jnp.repeat(scale_row(base_key, row_id // QBLOCK), QBLOCK)
    return (codes_row * scales_row).astype(jnp.bfloat16).astype(jnp.float32)


def draw_head_codes(key, part):
    values = jax.vmap(partial(code_row, key))(jnp.arange(VOCAB))
    return values.astype(jnp.bfloat16)


def draw_head_scales(key, part):
    return jax.vmap(partial(scale_row, key))(jnp.arange(VOCAB // QBLOCK))


def add_peaks(random_part, shared, peak_ids, heights):
    peak_rows = jax.vmap(partial(head_row, shared))(peak_ids)
    peak_norm = jnp.sum(peak_rows * peak_rows, axis=1)
    return random_part + (heights / peak_norm)[:, None] * peak_rows


def draw_hidden(key, part):
    shared = key
    key = jax.random.fold_in(key, 13)
    subkeys = jax.random.split(key, 9)
    unit_scale = 1.0 / math.sqrt(D * 0.00215)
    peak_ids = jax.random.randint(subkeys[7], (TOKENS,), 0, VOCAB)
    spread = jnp.exp(jax.random.uniform(subkeys[0], (TOKENS, 1), jnp.float32, math.log(0.6), math.log(1.2)))
    random_part = spread * unit_scale * jnp.clip(jax.random.normal(subkeys[2], (TOKENS, D), jnp.float32), -4.0, 4.0)
    heights = jax.random.uniform(subkeys[8], (TOKENS,), jnp.float32, 7.0, 8.0)
    values = add_peaks(random_part, shared, peak_ids, heights)
    return values.astype(jnp.bfloat16)


def setup_inputs(seed: int = 0, part: int = 0) -> dict:
    key_list = jax.random.split(jax.random.key(seed), 4)
    part_keys = jax.random.split(jax.random.fold_in(key_list[3], part), 4)
    hidden = draw_hidden(jax.random.fold_in(jax.random.fold_in(key_list[3], part), 71), part)
    head_codes = draw_head_codes(jax.random.fold_in(jax.random.fold_in(key_list[3], part), 71), part)
    head_scales = draw_head_scales(jax.random.fold_in(jax.random.fold_in(key_list[3], part), 71), part)
    return dict(hidden=hidden, head_codes=head_codes, head_scales=head_scales)


def dequant_block(block_codes, scales):
    model_width = block_codes.shape[1]
    grouped = block_codes.reshape(QBLOCK, model_width // QBLOCK, QBLOCK).astype(jnp.float32)
    return (grouped * scales[None, :, None]).reshape(QBLOCK, model_width).astype(jnp.bfloat16)


def reference(hidden, head_codes, head_scales):
    block_count = head_codes.shape[0] // QBLOCK
    code_blocks = head_codes.reshape(block_count, QBLOCK, D)

    def block_logits(block_pair):
        weight = dequant_block(block_pair[0], block_pair[1])
        return jnp.dot(hidden, weight.T, preferred_element_type=jnp.float32)

    stacked = lax.map(block_logits, (code_blocks, head_scales))
    token_count = hidden.shape[0]
    logits = jnp.transpose(stacked, (1, 0, 2)).reshape(token_count, block_count * QBLOCK)
    vocab_blocks = logits.reshape(token_count, N_VOCAB, V_DEV)
    block_top = jnp.max(vocab_blocks, axis=2)
    shifted = vocab_blocks - block_top[:, :, None]
    expon = jnp.exp(shifted)
    block_sum = jnp.sum(expon, axis=2)
    block_tilt = jnp.sum(expon * shifted, axis=2)
    block_exp = lax.optimization_barrier(expon.astype(jnp.bfloat16)).astype(jnp.float32)
    top_value = jnp.max(block_top, axis=1)
    factor = jnp.exp(block_top - top_value[:, None])
    exp_sum = jnp.sum(block_sum * factor, axis=1)
    tilt_sum = jnp.sum(factor * (block_tilt + block_sum * (block_top - top_value[:, None])), axis=1)
    scaled = block_exp * (factor / exp_sum[:, None])[:, :, None]
    probabilities = scaled.reshape(token_count, N_VOCAB * V_DEV).astype(jnp.bfloat16)
    entropy = jnp.log(exp_sum) - tilt_sum / exp_sum
    return probabilities, entropy
```

```python
import functools

import jax
import jax.numpy as jnp
from jax import lax
from jax.experimental import pallas as pl
from jax.experimental.pallas import tpu as pltpu
from jax.sharding import PartitionSpec as P

MESH = pl.DeviceIdType.MESH
BLOCK = 128
TILE = 256

SLOTS = [
    (0, 0), (0, 1), (0, 3), (1, 0), (3, 0), (1, 3), (3, 1), (1, 1), (3, 3),
    (0, 2), (2, 0), (1, 2), (3, 2), (2, 1), (2, 3), (2, 2),
]
SLOT = {chip: slot for slot, chip in enumerate(SLOTS)}
UP, DOWN = 1, 3


def axis_move(half, stage, step):
    along_y = (half == 0) == (stage == 0)
    return (0, step) if along_y else (step, 0)


def add(a, b):
    return ((a[0] + b[0]) % 4, (a[1] + b[1]) % 4)


def neg(a):
    return ((-a[0]) % 4, (-a[1]) % 4)


def piece_table():
    pieces = []
    for half in (0, 1):
        for chip in SLOTS[1:]:
            first, second = (chip[1], chip[0]) if half == 0 else (chip[0], chip[1])
            last = second if second else first
            pieces += [(half, chip, q) for q in ((0, 1) if last == 2 else (None,))]
    return {piece: i for i, piece in enumerate(pieces)}


PIECE = piece_table()


def head_kernel(
    rows, hidden, codes, scales, raw, stats_in,
    gathered, weight, staged, logits, expo, stats_out,
    copy_sem, stage_sem, ici_send, ici_recv, sib_send, sib_recv, out_send, out_recv, st_send, st_recv,
):
    width = hidden.shape[1]
    vocab = codes.shape[0]
    half_w, quarter_w = width // 2, width // 4
    me = lax.axis_index("vocab")
    z, y, c = me // 8, lax.rem(me // 2, 4), lax.rem(me, 2)

    def device(chip, core=0):
        index = (lax.rem(z + chip[0], 4) * 4 + lax.rem(y + chip[1], 4)) * 2 + lax.rem(c + core, 2)
        return {"vocab": index}

    def row_block(chip, core=0):
        return pl.ds(SLOT[chip] * 2 * rows + core * rows, rows)

    def columns(half, quarter=None):
        if quarter is None:
            return pl.ds(half * half_w, half_w)
        return pl.ds(half * half_w + quarter * quarter_w, quarter_w)

    def remote(src, dst, send, recv, target):
        pltpu.make_async_remote_copy(
            src_ref=src, dst_ref=dst, send_sem=send, recv_sem=recv, device_id=target, device_id_type=MESH
        ).start()

    def pass_on(half, chip, quarter, move):
        cols = columns(half, quarter)
        there = add(chip, neg(move))
        src = hidden.at[:, cols] if chip == (0, 0) else gathered.at[row_block(chip), cols]
        remote(
            src,
            gathered.at[row_block(there), cols],
            ici_send,
            ici_recv.at[PIECE[half, there, quarter]],
            device(move),
        )

    def arrived(half, chip, quarter=None):
        cols = columns(half, quarter)
        ref = gathered.at[row_block(chip), cols]
        pltpu.make_async_copy(ref, ref, ici_recv.at[PIECE[half, chip, quarter]]).wait()

    def share(half, chip):
        cols = columns(half)
        remote(
            gathered.at[row_block(chip), cols],
            gathered.at[row_block(chip, 1), cols],
            sib_send,
            sib_recv.at[SLOT[chip] * 2 + half],
            device((0, 0), 1),
        )

    def first_pair(half):
        up, down = axis_move(half, 0, UP), axis_move(half, 0, DOWN)
        arrived(half, up)
        arrived(half, down)
        pass_on(half, up, 1, down)
        pass_on(half, down, 0, up)
        up2, down2 = axis_move(half, 1, UP), axis_move(half, 1, DOWN)
        pass_on(half, up, None, up2)
        pass_on(half, down, None, down2)
        pass_on(half, up, None, down2)
        pass_on(half, down, None, up2)
        share(half, up)
        share(half, down)

    def first_opposite(half):
        chip = axis_move(half, 0, 2)
        arrived(half, chip, 0)
        arrived(half, chip, 1)
        pass_on(half, chip, None, axis_move(half, 1, UP))
        pass_on(half, chip, None, axis_move(half, 1, DOWN))
        share(half, chip)

    def second(half, first_step, direction):
        back = axis_move(half, 1, UP if direction == DOWN else DOWN)
        chip = add(axis_move(half, 0, first_step), axis_move(half, 1, direction))
        arrived(half, chip)
        pass_on(half, chip, 1 if direction == UP else 0, back)
        share(half, chip)

    def second_opposite(half, first_step):
        chip = add(axis_move(half, 0, first_step), axis_move(half, 1, 2))
        arrived(half, chip, 0)
        arrived(half, chip, 1)
        share(half, chip)

    barrier = pltpu.get_barrier_semaphore()
    neighbours = [device((0, UP)), device((0, DOWN)), device((UP, 0)), device((DOWN, 0)), device((0, 0), 1)]
    for neighbour in neighbours:
        pl.semaphore_signal(barrier, inc=1, device_id=neighbour, device_id_type=MESH)
    pl.semaphore_wait(barrier, len(neighbours))

    own = (0, 0)
    for stage in (0, 1):
        for half in (0, 1):
            for step in (UP, DOWN):
                pass_on(half, own, None, axis_move(half, stage, step))
    own_rows = gathered.at[row_block(own), :]
    remote(hidden, gathered.at[row_block(own, 1), :], sib_send, sib_recv.at[0], device(own, 1))
    own_copy = pltpu.make_async_copy(hidden, own_rows, copy_sem)
    own_copy.start()

    def stage_in(block):
        return pltpu.make_async_copy(
            codes.at[pl.ds(block * BLOCK, BLOCK), :], staged.at[block % 2], stage_sem.at[block % 2]
        )

    def dequantize(block):
        stage_in(block).wait()

        def body(i, carry):
            for j in range(4):
                d = i * 4 + j
                at = pl.ds(pl.multiple_of(d * BLOCK, BLOCK), BLOCK)
                tile = staged[block % 2, :, at].astype(jnp.float32) * scales[block, d]
                weight[at, pl.ds(block * BLOCK, BLOCK)] = tile.astype(jnp.bfloat16).T
            return carry

        lax.fori_loop(0, width // (4 * BLOCK), body, 0)
        if block + 2 < vocab // BLOCK:
            stage_in(block + 2).start()

    lane = lax.broadcasted_iota(jnp.int32, (rows, 128), 1)

    def compute(chips):
        base = SLOT[chips[0]] * 2 * rows
        count = len(chips) * 2 * rows
        for chip in chips:
            for half in (0, 1):
                if chip == own and half:
                    continue
                ref = gathered.at[row_block(chip, 1), pl.ds(0, width) if chip == own else columns(half)]
                pltpu.make_async_copy(ref, ref, sib_recv.at[SLOT[chip] * 2 + half]).wait()

        def body(i, carry):
            at = pl.ds(pl.multiple_of(i * TILE, TILE), TILE)
            logits[0:count, at] = jnp.dot(
                gathered[base : base + count, :], weight[:, at], preferred_element_type=jnp.float32
            )
            return carry

        lax.fori_loop(0, vocab // TILE, body, 0)
        for core in (0, 1):
            for i, chip in enumerate(chips):
                part = i * 2 + core
                value = logits[part * rows : (part + 1) * rows, :]
                top = jnp.max(value, axis=1, keepdims=True)
                shift = value - top
                expf = jnp.exp(shift)
                total = jnp.sum(expf, axis=1, keepdims=True)
                tilt = jnp.sum(expf * shift, axis=1, keepdims=True)
                at = row_block(chip, core)
                expo[at, :] = expf.astype(jnp.bfloat16)
                packed = jnp.where(lane == 0, top, jnp.where(lane == 1, total, tilt))
                packed = jnp.concatenate([packed, jnp.zeros((128 - rows, 128), jnp.float32)], axis=0)
                index = SLOT[chip] * 2 + core
                stats_out[index] = packed.T[0:8, :]
                there = raw.at[:, pl.ds(pl.multiple_of(me * vocab, vocab), vocab)]
                if chip == own and core == 0:
                    pltpu.make_async_copy(expo.at[at, :], there, out_recv).start()
                    pltpu.make_async_copy(stats_out.at[index], stats_in.at[me], st_recv).start()
                else:
                    remote(expo.at[at, :], there, out_send, out_recv, device(chip, core))
                    remote(stats_out.at[index], stats_in.at[me], st_send, st_recv, device(chip, core))

    stage_in(0).start()
    stage_in(1).start()
    for block in range(vocab // BLOCK):
        dequantize(block)
        if block == 3:
            first_pair(0)
            first_pair(1)
    for half in (0, 1):
        second(half, 0, UP)
        second(half, 0, DOWN)
    own_copy.wait()
    compute([own])
    first_opposite(0)
    first_opposite(1)
    compute([(0, 1), (0, 3)])
    for half in (0, 1):
        second(half, UP, DOWN)
        second(half, DOWN, UP)
    compute([(1, 0), (3, 0)])
    compute([(1, 3), (3, 1)])
    for half in (0, 1):
        second(half, UP, UP)
        second(half, DOWN, DOWN)
    compute([(1, 1), (3, 3)])
    second_opposite(0, 0)
    second_opposite(1, 0)
    compute([(0, 2), (2, 0)])
    for half in (0, 1):
        second(half, 2, UP)
        second(half, 2, DOWN)
    for half in (0, 1):
        second_opposite(half, UP)
        second_opposite(half, DOWN)
    compute([(1, 2), (3, 2)])
    compute([(2, 1), (2, 3)])
    second_opposite(0, 2)
    second_opposite(1, 2)
    compute([(2, 2)])

    def wait_bytes(ref, sem):
        pltpu.make_async_copy(ref, ref, sem).wait()

    wait_bytes(gathered.at[pl.ds(0, 15 * rows), :], ici_send)
    wait_bytes(gathered.at[pl.ds(0, 16 * rows), :], sib_send)
    wait_bytes(expo.at[pl.ds(0, 31 * rows), :], out_send)
    wait_bytes(stats_out.at[pl.ds(0, 31)], st_send)
    wait_bytes(raw, out_recv)
    wait_bytes(stats_in, st_recv)


def scale_kernel(rows, stats, raw, out, entropy, scale):
    blocks = stats.shape[0]
    step = pl.program_id(0)
    vocab = raw.shape[1] * pl.num_programs(0) // blocks
    per_step = raw.shape[1] // vocab

    @pl.when(step == 0)
    def _():
        top, total, tilt = stats[:, 0, :], stats[:, 1, :], stats[:, 2, :]
        top_value = jnp.max(top, axis=0, keepdims=True)
        factor = jnp.exp(top - top_value)
        exp_sum = jnp.sum(total * factor, axis=0, keepdims=True)
        tilt_sum = jnp.sum(factor * (tilt + total * (top - top_value)), axis=0, keepdims=True)
        entropy[...] = jnp.log(exp_sum) - tilt_sum / exp_sum
        ratio = factor / exp_sum
        ratio = jnp.concatenate([ratio, jnp.zeros((128 - blocks, 128), jnp.float32)], axis=0).T
        for s in range(blocks // per_step):
            scale[s] = ratio[0:rows, s * per_step : (s + 1) * per_step]

    ratio = scale[step]
    for b in range(per_step):
        at = slice(b * vocab, (b + 1) * vocab)
        out[:, at] = (raw[:, at].astype(jnp.float32) * ratio[:, b : b + 1]).astype(jnp.bfloat16)


def shards(n_vocab, hidden, head_codes, head_scales):
    rows, width = hidden.shape
    vocab = head_codes.shape[0]
    hbm, smem = pl.BlockSpec(memory_space=pl.ANY), pl.BlockSpec(memory_space=pltpu.SMEM)
    dma = pltpu.SemaphoreType.DMA
    raw, stats = pl.pallas_call(
        functools.partial(head_kernel, rows),
        out_shape=(
            jax.ShapeDtypeStruct((rows, n_vocab * vocab), jnp.bfloat16),
            jax.ShapeDtypeStruct((n_vocab, 8, 128), jnp.float32),
        ),
        in_specs=[hbm, hbm, smem],
        out_specs=(hbm, hbm),
        scratch_shapes=[
            pltpu.VMEM((n_vocab * rows, width), jnp.bfloat16),
            pltpu.VMEM((width, vocab), jnp.bfloat16),
            pltpu.VMEM((2, BLOCK, width), jnp.bfloat16),
            pltpu.VMEM((4 * rows, vocab), jnp.float32),
            pltpu.VMEM((n_vocab * rows, vocab), jnp.bfloat16),
            pltpu.VMEM((n_vocab, 8, 128), jnp.float32),
            dma, dma((2,)), dma, dma((len(PIECE),)), dma, dma((32,)), dma, dma, dma, dma,
        ],
        compiler_params=pltpu.CompilerParams(
            collective_id=0, has_side_effects=True, vmem_limit_bytes=60 << 20
        ),
        cost_estimate=pl.CostEstimate(
            flops=2 * n_vocab * rows * width * vocab,
            bytes_accessed=2 * vocab * width,
            transcendentals=n_vocab * rows * vocab,
        ),
        name="head",
    )(hidden, head_codes, head_scales)
    steps = 4
    cut = n_vocab * vocab // steps
    probabilities, entropy = pl.pallas_call(
        functools.partial(scale_kernel, rows),
        grid=(steps,),
        out_shape=(
            jax.ShapeDtypeStruct((rows, n_vocab * vocab), jnp.bfloat16),
            jax.ShapeDtypeStruct((1, 128), jnp.float32),
        ),
        in_specs=[
            pl.BlockSpec((n_vocab, 8, 128), lambda i: (0, 0, 0)),
            pl.BlockSpec((rows, cut), lambda i: (0, i)),
        ],
        out_specs=(pl.BlockSpec((rows, cut), lambda i: (0, i)), pl.BlockSpec((1, 128), lambda i: (0, 0))),
        scratch_shapes=[pltpu.VMEM((steps, rows, n_vocab // steps), jnp.float32)],
        compiler_params=pltpu.CompilerParams(vmem_limit_bytes=32 << 20),
        name="scale",
    )(stats, raw)
    return probabilities, entropy[0, :rows]


def solution(mesh):
    placed = P(("batch", "vocab"), None)
    return jax.shard_map(
        functools.partial(shards, mesh.shape["vocab"]),
        mesh=mesh,
        in_specs=(placed, placed, placed),
        out_specs=(placed, P(("batch", "vocab"))),
        check_vma=False,
    )
```

```python
import functools

import jax
import jax.numpy as jnp
from jax import lax
from jax.experimental import pallas as pl
from jax.experimental.pallas import tpu as pltpu
from jax.sharding import PartitionSpec as P

MESH = pl.DeviceIdType.MESH
BLOCK = 128
TILE = 256

STEPS = [
    [(0, 0)], [(0, 1), (0, 3)], [(1, 0), (3, 0)], [(1, 3), (3, 1)], [(1, 1), (3, 3)],
    [(0, 2), (2, 0)], [(1, 2), (2, 1)], [(3, 2), (2, 3)], [(2, 2)],
]
SLOTS = [chip for chips in STEPS for chip in chips]
SLOT = {chip: slot for slot, chip in enumerate(SLOTS)}
def add(a, b):
    return ((a[0] + b[0]) % 4, (a[1] + b[1]) % 4)


def neg(a):
    return ((-a[0]) % 4, (-a[1]) % 4)


def link_sends(along_y, step):
    first, second = (0, 1) if along_y else (1, 0)
    quarter = 0 if step == 1 else 1

    def chip(other, this):
        return (other % 4, this % 4) if along_y else (this % 4, other % 4)

    return [
        (first, chip(0, 0), None),
        (second, chip(0, 0), None),
        (first, chip(0, -step), quarter),
        (second, chip(step, 0), None),
        (second, chip(-step, 0), None),
        (second, chip(0, -step), quarter),
        (second, chip(2, 0), None),
        (second, chip(1, -step), quarter),
        (second, chip(-1, -step), quarter),
        (second, chip(2, -step), quarter),
    ]


LINKS = [(move, link_sends(move[0] == 0, sum(move))) for move in ((0, 1), (0, -1), (1, 0), (-1, 0))]
ROUNDS = 10
AHEAD = 3

def head_kernel(
    rows, hidden, codes, scales_in, raw, stats_in,
    scales, gathered, weight, staged, logits, expo, stats_out,
    scale_sem, copy_sem, stage_sem, ici_send, ici_recv, sib_send, sib_recv, out_send, out_recv, st_send, st_recv,
):
    width = hidden.shape[1]
    vocab = codes.shape[0]
    half_w, quarter_w = width // 2, width // 4
    me = lax.axis_index("vocab")
    z, y, c = me // 8, lax.rem(me // 2, 4), lax.rem(me, 2)

    def device(chip, core=0):
        index = (lax.rem(z + chip[0] % 4, 4) * 4 + lax.rem(y + chip[1] % 4, 4)) * 2 + lax.rem(c + core, 2)
        return {"vocab": index}

    def row_block(chip, core=0):
        return pl.ds(SLOT[chip] * 2 * rows + core * rows, rows)

    def columns(half, quarter=None):
        if quarter is None:
            return pl.ds(half * half_w, half_w)
        return pl.ds(half * half_w + quarter * quarter_w, quarter_w)

    def remote(src, dst, send, recv, target):
        pltpu.make_async_remote_copy(
            src_ref=src, dst_ref=dst, send_sem=send, recv_sem=recv, device_id=target, device_id_type=MESH
        ).start()

    def send(turn):
        for link, (move, sends) in enumerate(LINKS):
            half, chip, quarter = sends[turn]
            cols = columns(half, quarter)
            src = hidden.at[:, cols] if chip == (0, 0) else gathered.at[row_block(chip), cols]
            dst = gathered.at[row_block(add(chip, neg(move))), cols]
            remote(src, dst, ici_send, ici_recv.at[link * ROUNDS + turn], device(move))

    def receive(turn):
        halves = []
        for link, (move, sends) in enumerate(LINKS):
            half, chip, quarter = sends[turn]
            chip = add(chip, neg(move))
            ref = gathered.at[row_block(chip), columns(half, quarter)]
            pltpu.make_async_copy(ref, ref, ici_recv.at[link * ROUNDS + turn]).wait()
            if (half, chip) not in halves:
                halves.append((half, chip))
        if turn == 0:
            for early in range(2, AHEAD):
                send(early)
        if turn + AHEAD < ROUNDS:
            send(turn + AHEAD)
        for half, chip in halves:
            at = columns(half)
            remote(
                gathered.at[row_block(chip), at],
                gathered.at[row_block(chip, 1), at],
                sib_send,
                sib_recv.at[SLOT[chip] * 2 + half],
                device((0, 0), 1),
            )

    scale_copy = pltpu.make_async_copy(scales_in, scales, scale_sem)
    scale_copy.start()

    barrier = pltpu.get_barrier_semaphore()
    neighbours = [device(move) for move, _ in LINKS] + [device((0, 0), 1)]
    for neighbour in neighbours:
        pl.semaphore_signal(barrier, inc=1, device_id=neighbour, device_id_type=MESH)
    pl.semaphore_wait(barrier, len(neighbours))

    own = (0, 0)
    send(0)
    send(1)
    own_rows = gathered.at[row_block(own), :]
    remote(hidden, gathered.at[row_block(own, 1), :], sib_send, sib_recv.at[0], device(own, 1))
    own_copy = pltpu.make_async_copy(hidden, own_rows, copy_sem)
    own_copy.start()

    def stage_in(block):
        return pltpu.make_async_copy(
            codes.at[pl.ds(block * BLOCK, BLOCK), :], staged.at[block % 2], stage_sem.at[block % 2]
        )

    def dequantize(block):
        stage_in(block).wait()

        def body(i, carry):
            for j in range(4):
                d = i * 4 + j
                at = pl.ds(pl.multiple_of(d * BLOCK, BLOCK), BLOCK)
                tile = staged[block % 2, :, at].astype(jnp.float32) * scales[block, d]
                weight[at, pl.ds(block * BLOCK, BLOCK)] = tile.astype(jnp.bfloat16).T
            return carry

        lax.fori_loop(0, width // (4 * BLOCK), body, 0)
        if block + 2 < vocab // BLOCK:
            stage_in(block + 2).start()

    lane = lax.broadcasted_iota(jnp.int32, (rows, 128), 1)

    def compute(chips):
        base = SLOT[chips[0]] * 2 * rows
        count = len(chips) * 2 * rows
        for chip in chips:
            for half in (0, 1):
                if chip == own and half:
                    continue
                ref = gathered.at[row_block(chip, 1), pl.ds(0, width) if chip == own else columns(half)]
                pltpu.make_async_copy(ref, ref, sib_recv.at[SLOT[chip] * 2 + half]).wait()

        def body(i, carry):
            at = pl.ds(pl.multiple_of(i * TILE, TILE), TILE)
            logits[0:count, at] = jnp.dot(
                gathered[base : base + count, :], weight[:, at], preferred_element_type=jnp.float32
            )
            return carry

        lax.fori_loop(0, vocab // TILE, body, 0)
        for core in (0, 1):
            for i, chip in enumerate(chips):
                part = i * 2 + core
                value = logits[part * rows : (part + 1) * rows, :]
                top = jnp.max(value, axis=1, keepdims=True)
                shift = value - top
                expf = jnp.exp(shift)
                total = jnp.sum(expf, axis=1, keepdims=True)
                tilt = jnp.sum(expf * shift, axis=1, keepdims=True)
                at = row_block(chip, core)
                expo[at, :] = expf.astype(jnp.bfloat16)
                packed = jnp.where(lane == 0, top, jnp.where(lane == 1, total, tilt))
                packed = jnp.concatenate([packed, jnp.zeros((128 - rows, 128), jnp.float32)], axis=0)
                index = SLOT[chip] * 2 + core
                turned = packed.T
                for k in range(3):
                    stats_out[index, :, k * 128 : (k + 1) * 128] = turned[k : k + 1, :]
                there = raw.at[:, pl.ds(pl.multiple_of(me * vocab, vocab), vocab)]
                if chip == own and core == 0:
                    pltpu.make_async_copy(expo.at[at, :], there, out_recv).start()
                    pltpu.make_async_copy(stats_out.at[index], stats_in.at[me], st_recv).start()
                else:
                    remote(expo.at[at, :], there, out_send, out_recv, device(chip, core))
                    remote(stats_out.at[index], stats_in.at[me], st_send, st_recv, device(chip, core))

    stage_in(0).start()
    stage_in(1).start()
    scale_copy.wait()
    for block in range(vocab // BLOCK):
        dequantize(block)
        if block == 3:
            receive(0)
    receive(1)
    own_copy.wait()
    compute(STEPS[0])
    compute(STEPS[1])
    receive(2)
    compute(STEPS[2])
    receive(3)
    compute(STEPS[3])
    receive(4)
    compute(STEPS[4])
    receive(5)
    compute(STEPS[5])
    receive(6)
    receive(7)
    compute(STEPS[6])
    receive(8)
    compute(STEPS[7])
    receive(9)
    compute(STEPS[8])

    def wait_bytes(ref, sem):
        pltpu.make_async_copy(ref, ref, sem).wait()

    wait_bytes(gathered.at[pl.ds(0, 15 * rows), :], ici_send)
    wait_bytes(gathered.at[pl.ds(0, 16 * rows), :], sib_send)
    wait_bytes(expo.at[pl.ds(0, 31 * rows), :], out_send)
    wait_bytes(stats_out.at[pl.ds(0, 31)], st_send)
    wait_bytes(raw, out_recv)
    wait_bytes(stats_in, st_recv)


def scale_kernel(rows, per_step, stats, raw, out, entropy, ready, sems):
    blocks = stats.shape[0]
    vocab = raw.shape[1] // blocks
    top, total, tilt = stats[:, 0, 0:128], stats[:, 0, 128:256], stats[:, 0, 256:384]
    top_value = jnp.max(top, axis=0, keepdims=True)
    factor = jnp.exp(top - top_value)
    exp_sum = jnp.sum(total * factor, axis=0, keepdims=True)
    tilt_sum = jnp.sum(factor * (tilt + total * (top - top_value)), axis=0, keepdims=True)
    entropy[...] = (jnp.log(exp_sum) - tilt_sum / exp_sum)[0, 0:rows]
    ratio = factor / exp_sum
    ratio = jnp.concatenate([ratio, jnp.zeros((128 - blocks, 128), jnp.float32)], axis=0).T[0:rows]
    copies = []
    for step in range(blocks // per_step):
        cols = pl.ds(step * per_step * vocab, per_step * vocab)
        for b in range(step * per_step, (step + 1) * per_step):
            at = slice(b * vocab, (b + 1) * vocab)
            ready[:, at] = (raw[:, at].astype(jnp.float32) * ratio[:, b : b + 1]).astype(jnp.bfloat16)
        copies.append(pltpu.make_async_copy(ready.at[:, cols], out.at[:, cols], sems.at[step]))
        copies[-1].start()
    for copy in copies:
        copy.wait()


def shards(n_vocab, hidden, head_codes, head_scales):
    rows, width = hidden.shape
    vocab = head_codes.shape[0]
    hbm = pl.BlockSpec(memory_space=pltpu.HBM)
    vmem = pl.BlockSpec(memory_space=pltpu.VMEM)
    dma = pltpu.SemaphoreType.DMA
    raw, stats = pl.pallas_call(
        functools.partial(head_kernel, rows),
        out_shape=(
            jax.ShapeDtypeStruct((rows, n_vocab * vocab), jnp.bfloat16),
            jax.ShapeDtypeStruct((n_vocab, 1, 384), jnp.float32),
        ),
        in_specs=[hbm, hbm, hbm],
        out_specs=(vmem, vmem),
        scratch_shapes=[
            pltpu.SMEM(head_scales.shape, jnp.float32),
            pltpu.VMEM((n_vocab * rows, width), jnp.bfloat16),
            pltpu.VMEM((width, vocab), jnp.bfloat16),
            pltpu.VMEM((2, BLOCK, width), jnp.bfloat16),
            pltpu.VMEM((4 * rows, vocab), jnp.float32),
            pltpu.VMEM((n_vocab * rows, vocab), jnp.bfloat16),
            pltpu.VMEM((n_vocab, 1, 384), jnp.float32),
            dma, dma, dma((2,)), dma, dma((len(LINKS) * ROUNDS,)), dma, dma((32,)), dma, dma, dma, dma,
        ],
        compiler_params=pltpu.CompilerParams(
            collective_id=0, has_side_effects=True, vmem_limit_bytes=50 << 20
        ),
        cost_estimate=pl.CostEstimate(
            flops=2 * n_vocab * rows * width * vocab,
            bytes_accessed=2 * vocab * width,
            transcendentals=n_vocab * rows * vocab,
        ),
        name="head",
    )(*(pltpu.with_memory_space_constraint(x, pltpu.HBM) for x in (hidden, head_codes, head_scales)))
    steps = 8
    probabilities, entropy = pl.pallas_call(
        functools.partial(scale_kernel, rows, n_vocab // steps),
        out_shape=(
            jax.ShapeDtypeStruct((rows, n_vocab * vocab), jnp.bfloat16),
            jax.ShapeDtypeStruct((rows,), jnp.float32),
        ),
        in_specs=[vmem, vmem],
        out_specs=(hbm, vmem),
        scratch_shapes=[pltpu.VMEM((rows, n_vocab * vocab), jnp.bfloat16), dma((steps,))],
        compiler_params=pltpu.CompilerParams(vmem_limit_bytes=16 << 20),
        name="scale",
    )(stats, raw)
    return probabilities, entropy


def solution(mesh):
    placed = P(("batch", "vocab"), None)
    return jax.shard_map(
        functools.partial(shards, mesh.shape["vocab"]),
        mesh=mesh,
        in_specs=(placed, placed, placed),
        out_specs=(placed, P(("batch", "vocab"))),
        check_vma=False,
    )
```

```python
import functools

import jax
import jax.numpy as jnp
from jax import lax
from jax.experimental import pallas as pl
from jax.experimental.pallas import tpu as pltpu
from jax.sharding import PartitionSpec as P

MESH = pl.DeviceIdType.MESH
BLOCK = 128
TILE = 256

STEPS = [
    [(0, 0)], [(0, 1), (0, 3)], [(1, 0), (3, 0)], [(1, 3), (3, 1)], [(1, 1), (3, 3)],
    [(0, 2), (2, 0)], [(1, 2), (2, 1)], [(3, 2), (2, 3)], [(2, 2)],
]
SLOTS = [chip for chips in STEPS for chip in chips]
SLOT = {chip: slot for slot, chip in enumerate(SLOTS)}
def add(a, b):
    return ((a[0] + b[0]) % 4, (a[1] + b[1]) % 4)


def neg(a):
    return ((-a[0]) % 4, (-a[1]) % 4)


def link_sends(along_y, step):
    first, second = (0, 1) if along_y else (1, 0)
    quarter = 0 if step == 1 else 1

    def chip(other, this):
        return (other % 4, this % 4) if along_y else (this % 4, other % 4)

    return [
        (first, chip(0, 0), None),
        (second, chip(0, 0), None),
        (first, chip(0, -step), quarter),
        (second, chip(step, 0), None),
        (second, chip(-step, 0), None),
        (second, chip(0, -step), quarter),
        (second, chip(2, 0), None),
        (second, chip(1, -step), quarter),
        (second, chip(-1, -step), quarter),
        (second, chip(2, -step), quarter),
    ]


LINKS = [(move, link_sends(move[0] == 0, sum(move))) for move in ((0, 1), (0, -1), (1, 0), (-1, 0))]
ROUNDS = 10
AHEAD = 4


def send_turns():
    here = {}
    for move, sends in LINKS:
        for turn, (half, chip, _) in enumerate(sends):
            piece = (half, add(chip, neg(move)))
            here[piece] = max(turn, here.get(piece, 0))
    return [
        [max(here.get((half, chip), -1), turn - AHEAD if turn > 1 else -1) for turn, (half, chip, _) in enumerate(sends)]
        for _, sends in LINKS
    ]


SEND_TURNS = send_turns()

def head_kernel(
    rows, hidden, codes, scales_in, raw, ratio, entropy,
    scales, stats_in, gathered, weight, staged, logits, expo, stats_out,
    scale_sem, copy_sem, stage_sem, ici_send, ici_recv, sib_send, sib_recv, out_send, out_recv, st_send, st_recv,
):
    width = hidden.shape[1]
    vocab = codes.shape[0]
    half_w, quarter_w = width // 2, width // 4
    me = lax.axis_index("vocab")
    z, y, c = me // 8, lax.rem(me // 2, 4), lax.rem(me, 2)

    def device(chip, core=0):
        index = (lax.rem(z + chip[0] % 4, 4) * 4 + lax.rem(y + chip[1] % 4, 4)) * 2 + lax.rem(c + core, 2)
        return {"vocab": index}

    def row_block(chip, core=0):
        return pl.ds(SLOT[chip] * 2 * rows + core * rows, rows)

    def columns(half, quarter=None):
        if quarter is None:
            return pl.ds(half * half_w, half_w)
        return pl.ds(half * half_w + quarter * quarter_w, quarter_w)

    def remote(src, dst, send, recv, target):
        pltpu.make_async_remote_copy(
            src_ref=src, dst_ref=dst, send_sem=send, recv_sem=recv, device_id=target, device_id_type=MESH
        ).start()

    def send(after):
        for turn in range(ROUNDS):
            for link, (move, sends) in enumerate(LINKS):
                if SEND_TURNS[link][turn] != after:
                    continue
                half, chip, quarter = sends[turn]
                cols = columns(half, quarter)
                src = hidden.at[:, cols] if chip == (0, 0) else gathered.at[row_block(chip), cols]
                dst = gathered.at[row_block(add(chip, neg(move))), cols]
                remote(src, dst, ici_send, ici_recv.at[link * ROUNDS + turn], device(move))

    def receive(turn):
        halves = []
        for link, (move, sends) in enumerate(LINKS):
            half, chip, quarter = sends[turn]
            chip = add(chip, neg(move))
            ref = gathered.at[row_block(chip), columns(half, quarter)]
            pltpu.make_async_copy(ref, ref, ici_recv.at[link * ROUNDS + turn]).wait()
            if (half, chip) not in halves:
                halves.append((half, chip))
        send(turn)
        for half, chip in halves:
            at = columns(half)
            remote(
                gathered.at[row_block(chip), at],
                gathered.at[row_block(chip, 1), at],
                sib_send,
                sib_recv.at[SLOT[chip] * 2 + half],
                device((0, 0), 1),
            )

    scale_copy = pltpu.make_async_copy(scales_in, scales, scale_sem)
    scale_copy.start()

    barrier = pltpu.get_barrier_semaphore()
    neighbours = [device(move) for move, _ in LINKS] + [device((0, 0), 1)]
    for neighbour in neighbours:
        pl.semaphore_signal(barrier, inc=1, device_id=neighbour, device_id_type=MESH)
    pl.semaphore_wait(barrier, len(neighbours))

    own = (0, 0)
    send(-1)
    own_rows = gathered.at[row_block(own), :]
    remote(hidden, gathered.at[row_block(own, 1), :], sib_send, sib_recv.at[0], device(own, 1))
    own_copy = pltpu.make_async_copy(hidden, own_rows, copy_sem)
    own_copy.start()

    def stage_in(block):
        return pltpu.make_async_copy(
            codes.at[pl.ds(block * BLOCK, BLOCK), :], staged.at[block % 2], stage_sem.at[block % 2]
        )

    def dequantize(block):
        stage_in(block).wait()

        def body(i, carry):
            for j in range(4):
                d = i * 4 + j
                at = pl.ds(pl.multiple_of(d * BLOCK, BLOCK), BLOCK)
                tile = staged[block % 2, :, at].astype(jnp.float32) * scales[block, d]
                weight[at, pl.ds(block * BLOCK, BLOCK)] = tile.astype(jnp.bfloat16).T
            return carry

        lax.fori_loop(0, width // (4 * BLOCK), body, 0)
        if block + 2 < vocab // BLOCK:
            stage_in(block + 2).start()

    lane = lax.broadcasted_iota(jnp.int32, (rows, 128), 1)

    def deliver(chip, core):
        index = SLOT[chip] * 2 + core
        block, stats = expo.at[row_block(chip, core), :], stats_out.at[index]
        there = raw.at[:, pl.ds(pl.multiple_of(me * vocab, vocab), vocab)]
        if chip == own and core == 0:
            pltpu.make_async_copy(block, there, out_recv).start()
            pltpu.make_async_copy(stats, stats_in.at[me], st_recv).start()
        else:
            remote(stats, stats_in.at[me], st_send, st_recv, device(chip, core))
            remote(block, there, out_send, out_recv, device(chip, core))

    def deliver_all(chips):
        for core in (0, 1):
            for chip in chips:
                deliver(chip, core)

    def compute(chips, send_now=True):
        base = SLOT[chips[0]] * 2 * rows
        count = len(chips) * 2 * rows
        for chip in chips:
            for half in (0, 1):
                if chip == own and half:
                    continue
                ref = gathered.at[row_block(chip, 1), pl.ds(0, width) if chip == own else columns(half)]
                pltpu.make_async_copy(ref, ref, sib_recv.at[SLOT[chip] * 2 + half]).wait()

        def body(i, carry):
            at = pl.ds(pl.multiple_of(i * TILE, TILE), TILE)
            logits[0:count, at] = jnp.dot(
                gathered[base : base + count, :], weight[:, at], preferred_element_type=jnp.float32
            )
            return carry

        lax.fori_loop(0, vocab // TILE, body, 0)
        for core in (0, 1):
            for i, chip in enumerate(chips):
                part = i * 2 + core
                value = logits[part * rows : (part + 1) * rows, :]
                top = jnp.max(value, axis=1, keepdims=True)
                shift = value - top
                expf = jnp.exp(shift)
                total = jnp.sum(expf, axis=1, keepdims=True)
                tilt = jnp.sum(expf * shift, axis=1, keepdims=True)
                at = row_block(chip, core)
                expo[at, :] = expf.astype(jnp.bfloat16)
                packed = jnp.where(lane == 0, top, jnp.where(lane == 1, total, tilt))
                packed = jnp.concatenate([packed, jnp.zeros((128 - rows, 128), jnp.float32)], axis=0)
                index = SLOT[chip] * 2 + core
                turned = packed.T
                for k in range(3):
                    stats_out[index, :, k * 128 : (k + 1) * 128] = turned[k : k + 1, :]
                if send_now:
                    deliver(chip, core)

    stage_in(0).start()
    stage_in(1).start()
    scale_copy.wait()
    for block in range(vocab // BLOCK):
        dequantize(block)
        if block == 3:
            receive(0)
    receive(1)
    own_copy.wait()
    compute(STEPS[0], False)
    compute(STEPS[1], False)
    receive(2)
    compute(STEPS[2], False)
    receive(3)
    compute(STEPS[3])
    receive(4)
    compute(STEPS[4])
    receive(5)
    compute(STEPS[5])
    receive(6)
    receive(7)
    compute(STEPS[6])
    deliver_all([chip for pair in zip(STEPS[1], STEPS[2]) for chip in pair])
    receive(8)
    compute(STEPS[7])
    receive(9)
    deliver_all(STEPS[0])
    compute(STEPS[8])

    def wait_bytes(ref, sem):
        pltpu.make_async_copy(ref, ref, sem).wait()

    wait_bytes(gathered.at[pl.ds(0, 15 * rows), :], ici_send)
    wait_bytes(gathered.at[pl.ds(0, 16 * rows), :], sib_send)
    wait_bytes(expo.at[pl.ds(0, 31 * rows), :], out_send)
    wait_bytes(stats_out.at[pl.ds(0, 31)], st_send)
    wait_bytes(stats_in, st_recv)
    blocks = stats_in.shape[0]
    top, total, tilt = (stats_in[:, 0, k * 128 : (k + 1) * 128] for k in range(3))
    top_value = jnp.max(top, axis=0, keepdims=True)
    factor = jnp.exp(top - top_value)
    exp_sum = jnp.sum(total * factor, axis=0, keepdims=True)
    tilt_sum = jnp.sum(factor * (tilt + total * (top - top_value)), axis=0, keepdims=True)
    entropy[...] = jnp.log(exp_sum) - tilt_sum / exp_sum
    share_of_sum = jnp.concatenate([factor / exp_sum, jnp.zeros((128 - blocks, 128), jnp.float32)], axis=0)
    ratio[...] = share_of_sum.T[0:rows]
    wait_bytes(raw, out_recv)


def scale_kernel(rows, per_step, blocks, entropy_in, ratio, raw, out, entropy, ready, sems):
    vocab = raw.shape[1] // blocks
    entropy[...] = entropy_in[0, 0:rows]
    copies = []
    for step in range(blocks // per_step):
        cols = pl.ds(step * per_step * vocab, per_step * vocab)
        for b in range(step * per_step, (step + 1) * per_step):
            at = slice(b * vocab, (b + 1) * vocab)
            ready[:, at] = (raw[:, at].astype(jnp.float32) * ratio[:, b : b + 1]).astype(jnp.bfloat16)
        copies.append(pltpu.make_async_copy(ready.at[:, cols], out.at[:, cols], sems.at[step]))
        copies[-1].start()
    for copy in copies:
        copy.wait()


def shards(n_vocab, hidden, head_codes, head_scales):
    rows, width = hidden.shape
    vocab = head_codes.shape[0]
    hbm = pl.BlockSpec(memory_space=pltpu.HBM)
    vmem = pl.BlockSpec(memory_space=pltpu.VMEM)
    dma = pltpu.SemaphoreType.DMA
    raw, ratio, entropy = pl.pallas_call(
        functools.partial(head_kernel, rows),
        out_shape=(
            jax.ShapeDtypeStruct((rows, n_vocab * vocab), jnp.bfloat16),
            jax.ShapeDtypeStruct((rows, 128), jnp.float32),
            jax.ShapeDtypeStruct((1, 128), jnp.float32),
        ),
        in_specs=[hbm, hbm, hbm],
        out_specs=(vmem, vmem, vmem),
        scratch_shapes=[
            pltpu.SMEM(head_scales.shape, jnp.float32),
            pltpu.VMEM((n_vocab, 1, 384), jnp.float32),
            pltpu.VMEM((n_vocab * rows, width), jnp.bfloat16),
            pltpu.VMEM((width, vocab), jnp.bfloat16),
            pltpu.VMEM((2, BLOCK, width), jnp.bfloat16),
            pltpu.VMEM((4 * rows, vocab), jnp.float32),
            pltpu.VMEM((n_vocab * rows, vocab), jnp.bfloat16),
            pltpu.VMEM((n_vocab, 1, 384), jnp.float32),
            dma, dma, dma((2,)), dma, dma((len(LINKS) * ROUNDS,)), dma, dma((32,)), dma, dma, dma, dma,
        ],
        compiler_params=pltpu.CompilerParams(
            collective_id=0, has_side_effects=True, vmem_limit_bytes=50 << 20
        ),
        cost_estimate=pl.CostEstimate(
            flops=2 * n_vocab * rows * width * vocab,
            bytes_accessed=2 * vocab * width,
            transcendentals=n_vocab * rows * vocab,
        ),
        name="head",
    )(*(pltpu.with_memory_space_constraint(x, pltpu.HBM) for x in (hidden, head_codes, head_scales)))
    steps = 8
    probabilities, entropy = pl.pallas_call(
        functools.partial(scale_kernel, rows, n_vocab // steps, n_vocab),
        out_shape=(
            jax.ShapeDtypeStruct((rows, n_vocab * vocab), jnp.bfloat16),
            jax.ShapeDtypeStruct((rows,), jnp.float32),
        ),
        in_specs=[vmem, vmem, vmem],
        out_specs=(hbm, vmem),
        scratch_shapes=[pltpu.VMEM((rows, n_vocab * vocab), jnp.bfloat16), dma((steps,))],
        compiler_params=pltpu.CompilerParams(vmem_limit_bytes=16 << 20),
        name="scale",
    )(entropy, ratio, raw)
    return probabilities, entropy


def solution(mesh):
    placed = P(("batch", "vocab"), None)
    return jax.shard_map(
        functools.partial(shards, mesh.shape["vocab"]),
        mesh=mesh,
        in_specs=(placed, placed, placed),
        out_specs=(placed, P(("batch", "vocab"))),
        check_vma=False,
    )
```

```python
import functools

import jax
import jax.numpy as jnp
from jax import lax
from jax.experimental import pallas as pl
from jax.experimental.pallas import tpu as pltpu
from jax.sharding import PartitionSpec as P

MESH = pl.DeviceIdType.MESH
BLOCK = 128
TILE = 256

STEPS = [
    [(0, 0)], [(0, 1), (0, 3)], [(1, 0), (3, 0)], [(1, 3), (3, 1)], [(1, 1), (3, 3)],
    [(0, 2), (2, 0)], [(1, 2), (2, 1)], [(3, 2), (2, 3)], [(2, 2)],
]
SLOTS = [chip for chips in STEPS for chip in chips]
SLOT = {chip: slot for slot, chip in enumerate(SLOTS)}
def add(a, b):
    return ((a[0] + b[0]) % 4, (a[1] + b[1]) % 4)


def neg(a):
    return ((-a[0]) % 4, (-a[1]) % 4)


def link_sends(along_y, step):
    first, second = (0, 1) if along_y else (1, 0)
    quarter = 0 if step == 1 else 1

    def chip(other, this):
        return (other % 4, this % 4) if along_y else (this % 4, other % 4)

    return [
        (first, chip(0, 0), None),
        (second, chip(0, 0), None),
        (first, chip(0, -step), quarter),
        (second, chip(step, 0), None),
        (second, chip(-step, 0), None),
        (second, chip(0, -step), quarter),
        (second, chip(2, 0), None),
        (second, chip(1, -step), quarter),
        (second, chip(-1, -step), quarter),
        (second, chip(2, -step), quarter),
    ]


LINKS = [(move, link_sends(move[0] == 0, sum(move))) for move in ((0, 1), (0, -1), (1, 0), (-1, 0))]
ROUNDS = 10
AHEAD = 4


def send_turns():
    here = {}
    for move, sends in LINKS:
        for turn, (half, chip, _) in enumerate(sends):
            piece = (half, add(chip, neg(move)))
            here[piece] = max(turn, here.get(piece, 0))
    return [
        [max(here.get((half, chip), -1), turn - AHEAD if turn > 1 else -1) for turn, (half, chip, _) in enumerate(sends)]
        for _, sends in LINKS
    ]


SEND_TURNS = send_turns()

def head_kernel(
    rows, hidden, codes, scales_in, raw, ratio, entropy,
    scales, stats_in, gathered, weight, staged, logits, expo, stats_out,
    scale_sem, copy_sem, stage_sem, ici_send, ici_recv, sib_send, sib_recv, out_send, out_recv, st_send, st_recv,
):
    width = hidden.shape[1]
    vocab = codes.shape[0]
    half_w, quarter_w = width // 2, width // 4
    me = lax.axis_index("vocab")
    z, y, c = me // 8, lax.rem(me // 2, 4), lax.rem(me, 2)

    def device(chip, core=0):
        index = (lax.rem(z + chip[0] % 4, 4) * 4 + lax.rem(y + chip[1] % 4, 4)) * 2 + lax.rem(c + core, 2)
        return {"vocab": index}

    def row_block(chip, core=0):
        return pl.ds(SLOT[chip] * 2 * rows + core * rows, rows)

    def columns(half, quarter=None):
        if quarter is None:
            return pl.ds(half * half_w, half_w)
        return pl.ds(half * half_w + quarter * quarter_w, quarter_w)

    def remote(src, dst, send, recv, target):
        pltpu.make_async_remote_copy(
            src_ref=src, dst_ref=dst, send_sem=send, recv_sem=recv, device_id=target, device_id_type=MESH
        ).start()

    def send(after):
        for turn in range(ROUNDS):
            for link, (move, sends) in enumerate(LINKS):
                if SEND_TURNS[link][turn] != after:
                    continue
                half, chip, quarter = sends[turn]
                cols = columns(half, quarter)
                src = gathered.at[row_block(chip), cols]
                dst = gathered.at[row_block(add(chip, neg(move))), cols]
                remote(src, dst, ici_send, ici_recv.at[link * ROUNDS + turn], device(move))

    def receive(turn):
        halves = []
        for link, (move, sends) in enumerate(LINKS):
            half, chip, quarter = sends[turn]
            chip = add(chip, neg(move))
            ref = gathered.at[row_block(chip), columns(half, quarter)]
            pltpu.make_async_copy(ref, ref, ici_recv.at[link * ROUNDS + turn]).wait()
            if (half, chip) not in halves:
                halves.append((half, chip))
        send(turn)
        for half, chip in halves:
            at = columns(half)
            remote(
                gathered.at[row_block(chip), at],
                gathered.at[row_block(chip, 1), at],
                sib_send,
                sib_recv.at[SLOT[chip] * 2 + half],
                device((0, 0), 1),
            )

    scale_copy = pltpu.make_async_copy(scales_in, scales, scale_sem)
    scale_copy.start()
    own = (0, 0)
    own_rows = gathered.at[row_block(own), :]
    own_copy = pltpu.make_async_copy(hidden, own_rows, copy_sem)
    own_copy.start()

    barrier = pltpu.get_barrier_semaphore()
    neighbours = [device(move) for move, _ in LINKS] + [device((0, 0), 1)]
    for neighbour in neighbours:
        pl.semaphore_signal(barrier, inc=1, device_id=neighbour, device_id_type=MESH)
    pl.semaphore_wait(barrier, len(neighbours))

    own_copy.wait()
    send(-1)
    remote(own_rows, gathered.at[row_block(own, 1), :], sib_send, sib_recv.at[0], device(own, 1))

    def stage_in(block):
        return pltpu.make_async_copy(
            codes.at[pl.ds(block * BLOCK, BLOCK), :], staged.at[block % 2], stage_sem.at[block % 2]
        )

    def dequantize(block):
        stage_in(block).wait()

        def body(i, carry):
            for j in range(4):
                d = i * 4 + j
                at = pl.ds(pl.multiple_of(d * BLOCK, BLOCK), BLOCK)
                tile = staged[block % 2, :, at].astype(jnp.float32) * scales[block, d]
                weight[at, pl.ds(block * BLOCK, BLOCK)] = tile.astype(jnp.bfloat16).T
            return carry

        lax.fori_loop(0, width // (4 * BLOCK), body, 0)
        if block + 2 < vocab // BLOCK:
            stage_in(block + 2).start()

    lane = lax.broadcasted_iota(jnp.int32, (rows, 128), 1)

    def deliver(chip, core):
        index = SLOT[chip] * 2 + core
        block, stats = expo.at[row_block(chip, core), :], stats_out.at[index]
        there = raw.at[:, pl.ds(pl.multiple_of(me * vocab, vocab), vocab)]
        if chip == own and core == 0:
            pltpu.make_async_copy(block, there, out_recv).start()
            pltpu.make_async_copy(stats, stats_in.at[me], st_recv).start()
        else:
            remote(stats, stats_in.at[me], st_send, st_recv, device(chip, core))
            remote(block, there, out_send, out_recv, device(chip, core))

    def deliver_all(chips):
        for core in (0, 1):
            for chip in chips:
                deliver(chip, core)

    def compute(chips, send_now=True):
        base = SLOT[chips[0]] * 2 * rows
        count = len(chips) * 2 * rows
        for chip in chips:
            for half in (0, 1):
                if chip == own and half:
                    continue
                ref = gathered.at[row_block(chip, 1), pl.ds(0, width) if chip == own else columns(half)]
                pltpu.make_async_copy(ref, ref, sib_recv.at[SLOT[chip] * 2 + half]).wait()

        def body(i, carry):
            at = pl.ds(pl.multiple_of(i * TILE, TILE), TILE)
            logits[0:count, at] = jnp.dot(
                gathered[base : base + count, :], weight[:, at], preferred_element_type=jnp.float32
            )
            return carry

        lax.fori_loop(0, vocab // TILE, body, 0)
        for core in (0, 1):
            for i, chip in enumerate(chips):
                part = i * 2 + core
                value = logits[part * rows : (part + 1) * rows, :]
                top = jnp.max(value, axis=1, keepdims=True)
                shift = value - top
                expf = jnp.exp(shift)
                total = jnp.sum(expf, axis=1, keepdims=True)
                tilt = jnp.sum(expf * shift, axis=1, keepdims=True)
                at = row_block(chip, core)
                expo[at, :] = expf.astype(jnp.bfloat16)
                packed = jnp.where(lane == 0, top, jnp.where(lane == 1, total, tilt))
                packed = jnp.concatenate([packed, jnp.zeros((128 - rows, 128), jnp.float32)], axis=0)
                index = SLOT[chip] * 2 + core
                turned = packed.T
                for k in range(3):
                    stats_out[index, :, k * 128 : (k + 1) * 128] = turned[k : k + 1, :]
                if send_now:
                    deliver(chip, core)

    stage_in(0).start()
    stage_in(1).start()
    scale_copy.wait()
    for block in range(vocab // BLOCK):
        dequantize(block)
        if block == 3:
            receive(0)
    receive(1)
    compute(STEPS[0], False)
    compute(STEPS[1], False)
    receive(2)
    compute(STEPS[2], False)
    receive(3)
    compute(STEPS[3])
    receive(4)
    compute(STEPS[4])
    receive(5)
    compute(STEPS[5])
    receive(6)
    receive(7)
    compute(STEPS[6])
    deliver_all([chip for pair in zip(STEPS[1], STEPS[2]) for chip in pair])
    receive(8)
    compute(STEPS[7])
    receive(9)
    deliver_all(STEPS[0])
    compute(STEPS[8])

    def wait_bytes(ref, sem):
        pltpu.make_async_copy(ref, ref, sem).wait()

    wait_bytes(gathered.at[pl.ds(0, 15 * rows), :], ici_send)
    wait_bytes(gathered.at[pl.ds(0, 16 * rows), :], sib_send)
    wait_bytes(expo.at[pl.ds(0, 31 * rows), :], out_send)
    wait_bytes(stats_out.at[pl.ds(0, 31)], st_send)
    wait_bytes(stats_in, st_recv)
    blocks = stats_in.shape[0]
    top, total, tilt = (stats_in[:, 0, k * 128 : (k + 1) * 128] for k in range(3))
    top_value = jnp.max(top, axis=0, keepdims=True)
    factor = jnp.exp(top - top_value)
    exp_sum = jnp.sum(total * factor, axis=0, keepdims=True)
    tilt_sum = jnp.sum(factor * (tilt + total * (top - top_value)), axis=0, keepdims=True)
    entropy[...] = jnp.log(exp_sum) - tilt_sum / exp_sum
    share_of_sum = jnp.concatenate([factor / exp_sum, jnp.zeros((128 - blocks, 128), jnp.float32)], axis=0)
    ratio[...] = share_of_sum.T[0:rows]
    wait_bytes(raw, out_recv)


def scale_kernel(rows, per_step, blocks, entropy_in, ratio, raw, out, entropy, ready, sems):
    vocab = raw.shape[1] // blocks
    entropy[...] = entropy_in[0, 0:rows]
    copies = []
    for step in range(blocks // per_step):
        cols = pl.ds(step * per_step * vocab, per_step * vocab)
        for b in range(step * per_step, (step + 1) * per_step):
            at = slice(b * vocab, (b + 1) * vocab)
            ready[:, at] = (raw[:, at].astype(jnp.float32) * ratio[:, b : b + 1]).astype(jnp.bfloat16)
        copies.append(pltpu.make_async_copy(ready.at[:, cols], out.at[:, cols], sems.at[step]))
        copies[-1].start()
    for copy in copies:
        copy.wait()


def shards(n_vocab, hidden, head_codes, head_scales):
    rows, width = hidden.shape
    vocab = head_codes.shape[0]
    hbm = pl.BlockSpec(memory_space=pltpu.HBM)
    vmem = pl.BlockSpec(memory_space=pltpu.VMEM)
    dma = pltpu.SemaphoreType.DMA
    raw, ratio, entropy = pl.pallas_call(
        functools.partial(head_kernel, rows),
        out_shape=(
            jax.ShapeDtypeStruct((rows, n_vocab * vocab), jnp.bfloat16),
            jax.ShapeDtypeStruct((rows, 128), jnp.float32),
            jax.ShapeDtypeStruct((1, 128), jnp.float32),
        ),
        in_specs=[hbm, hbm, hbm],
        out_specs=(vmem, vmem, vmem),
        scratch_shapes=[
            pltpu.SMEM(head_scales.shape, jnp.float32),
            pltpu.VMEM((n_vocab, 1, 384), jnp.float32),
            pltpu.VMEM((n_vocab * rows, width), jnp.bfloat16),
            pltpu.VMEM((width, vocab), jnp.bfloat16),
            pltpu.VMEM((2, BLOCK, width), jnp.bfloat16),
            pltpu.VMEM((4 * rows, vocab), jnp.float32),
            pltpu.VMEM((n_vocab * rows, vocab), jnp.bfloat16),
            pltpu.VMEM((n_vocab, 1, 384), jnp.float32),
            dma, dma, dma((2,)), dma, dma((len(LINKS) * ROUNDS,)), dma, dma((32,)), dma, dma, dma, dma,
        ],
        compiler_params=pltpu.CompilerParams(
            collective_id=0, has_side_effects=True, vmem_limit_bytes=50 << 20
        ),
        cost_estimate=pl.CostEstimate(
            flops=2 * n_vocab * rows * width * vocab,
            bytes_accessed=2 * vocab * width,
            transcendentals=n_vocab * rows * vocab,
        ),
        name="head",
    )(*(pltpu.with_memory_space_constraint(x, pltpu.HBM) for x in (hidden, head_codes, head_scales)))
    steps = 8
    probabilities, entropy = pl.pallas_call(
        functools.partial(scale_kernel, rows, n_vocab // steps, n_vocab),
        out_shape=(
            jax.ShapeDtypeStruct((rows, n_vocab * vocab), jnp.bfloat16),
            jax.ShapeDtypeStruct((rows,), jnp.float32),
        ),
        in_specs=[vmem, vmem, vmem],
        out_specs=(hbm, vmem),
        scratch_shapes=[pltpu.VMEM((rows, n_vocab * vocab), jnp.bfloat16), dma((steps,))],
        compiler_params=pltpu.CompilerParams(vmem_limit_bytes=16 << 20),
        name="scale",
    )(entropy, ratio, raw)
    return probabilities, entropy


def solution(mesh):
    placed = P(("batch", "vocab"), None)
    return jax.shard_map(
        functools.partial(shards, mesh.shape["vocab"]),
        mesh=mesh,
        in_specs=(placed, placed, placed),
        out_specs=(placed, P(("batch", "vocab"))),
        check_vma=False,
    )
```

```python
import functools

import jax
import jax.numpy as jnp
from jax import lax
from jax.experimental import pallas as pl
from jax.experimental.pallas import tpu as pltpu
from jax.sharding import PartitionSpec as P

MESH = pl.DeviceIdType.MESH
BLOCK = 128
TILE = 256

STEPS = [
    [(0, 0)], [(0, 1), (0, 3)], [(1, 0), (3, 0)], [(1, 3), (3, 1)], [(1, 1), (3, 3)],
    [(0, 2), (2, 0)], [(1, 2), (2, 1)], [(3, 2), (2, 3)], [(2, 2)],
]
SLOTS = [chip for chips in STEPS for chip in chips]
SLOT = {chip: slot for slot, chip in enumerate(SLOTS)}
def add(a, b):
    return ((a[0] + b[0]) % 4, (a[1] + b[1]) % 4)


def neg(a):
    return ((-a[0]) % 4, (-a[1]) % 4)


def link_sends(along_y, step):
    first, second = (0, 1) if along_y else (1, 0)
    quarter = 0 if step == 1 else 1

    def chip(other, this):
        return (other % 4, this % 4) if along_y else (this % 4, other % 4)

    return [
        (first, chip(0, 0), None),
        (second, chip(0, 0), None),
        (first, chip(0, -step), quarter),
        (second, chip(step, 0), None),
        (second, chip(-step, 0), None),
        (second, chip(0, -step), quarter),
        (second, chip(2, 0), None),
        (second, chip(1, -step), quarter),
        (second, chip(-1, -step), quarter),
        (second, chip(2, -step), quarter),
    ]


LINKS = [(move, link_sends(move[0] == 0, sum(move))) for move in ((0, 1), (0, -1), (1, 0), (-1, 0))]
ROUNDS = 10
AHEAD = 4


def send_turns():
    here = {}
    for move, sends in LINKS:
        for turn, (half, chip, _) in enumerate(sends):
            piece = (half, add(chip, neg(move)))
            here[piece] = max(turn, here.get(piece, 0))
    may = [
        [max(here.get((half, chip), -1), turn - AHEAD if turn > 1 else -1) for turn, (half, chip, _) in enumerate(sends)]
        for _, sends in LINKS
    ]
    return [[max(turns) for turns in zip(*may)]] * len(LINKS)


SEND_TURNS = send_turns()

def head_kernel(
    rows, hidden, codes, scales_in, raw, ratio, entropy,
    scales, stats_in, gathered, weight, staged, logits, expo, stats_out,
    scale_sem, copy_sem, stage_sem, ici_send, ici_recv, sib_send, sib_recv, out_send, out_recv, st_send, st_recv,
):
    width = hidden.shape[1]
    vocab = codes.shape[0]
    half_w, quarter_w = width // 2, width // 4
    me = lax.axis_index("vocab")
    z, y, c = me // 8, lax.rem(me // 2, 4), lax.rem(me, 2)

    def device(chip, core=0):
        index = (lax.rem(z + chip[0] % 4, 4) * 4 + lax.rem(y + chip[1] % 4, 4)) * 2 + lax.rem(c + core, 2)
        return {"vocab": index}

    def row_block(chip, core=0):
        return pl.ds(SLOT[chip] * 2 * rows + core * rows, rows)

    def columns(half, quarter=None):
        if quarter is None:
            return pl.ds(half * half_w, half_w)
        return pl.ds(half * half_w + quarter * quarter_w, quarter_w)

    def remote(src, dst, send, recv, target):
        pltpu.make_async_remote_copy(
            src_ref=src, dst_ref=dst, send_sem=send, recv_sem=recv, device_id=target, device_id_type=MESH
        ).start()

    def send(after):
        for turn in range(ROUNDS):
            for link, (move, sends) in enumerate(LINKS):
                if SEND_TURNS[link][turn] != after:
                    continue
                half, chip, quarter = sends[turn]
                cols = columns(half, quarter)
                src = gathered.at[row_block(chip), cols]
                dst = gathered.at[row_block(add(chip, neg(move))), cols]
                remote(src, dst, ici_send, ici_recv.at[link * ROUNDS + turn], device(move))

    def receive(turn):
        halves = []
        for link, (move, sends) in enumerate(LINKS):
            half, chip, quarter = sends[turn]
            chip = add(chip, neg(move))
            ref = gathered.at[row_block(chip), columns(half, quarter)]
            pltpu.make_async_copy(ref, ref, ici_recv.at[link * ROUNDS + turn]).wait()
            if (half, chip) not in halves:
                halves.append((half, chip))
        send(turn)
        for half, chip in halves:
            at = columns(half)
            remote(
                gathered.at[row_block(chip), at],
                gathered.at[row_block(chip, 1), at],
                sib_send,
                sib_recv.at[SLOT[chip] * 2 + half],
                device((0, 0), 1),
            )

    scale_copy = pltpu.make_async_copy(scales_in, scales, scale_sem)
    scale_copy.start()
    own = (0, 0)
    own_rows = gathered.at[row_block(own), :]
    own_copy = pltpu.make_async_copy(hidden, own_rows, copy_sem)
    own_copy.start()

    barrier = pltpu.get_barrier_semaphore()
    neighbours = [device(move) for move, _ in LINKS] + [device((0, 0), 1)]
    for neighbour in neighbours:
        pl.semaphore_signal(barrier, inc=1, device_id=neighbour, device_id_type=MESH)
    pl.semaphore_wait(barrier, len(neighbours))

    own_copy.wait()
    send(-1)
    remote(own_rows, gathered.at[row_block(own, 1), :], sib_send, sib_recv.at[0], device(own, 1))

    def stage_in(block):
        return pltpu.make_async_copy(
            codes.at[pl.ds(block * BLOCK, BLOCK), :], staged.at[block % 2], stage_sem.at[block % 2]
        )

    def dequantize(block):
        stage_in(block).wait()

        def body(i, carry):
            for j in range(4):
                d = i * 4 + j
                at = pl.ds(pl.multiple_of(d * BLOCK, BLOCK), BLOCK)
                tile = staged[block % 2, :, at].astype(jnp.float32) * scales[block, d]
                weight[at, pl.ds(block * BLOCK, BLOCK)] = tile.astype(jnp.bfloat16).T
            return carry

        lax.fori_loop(0, width // (4 * BLOCK), body, 0)
        if block + 2 < vocab // BLOCK:
            stage_in(block + 2).start()

    lane = lax.broadcasted_iota(jnp.int32, (rows, 128), 1)

    def deliver(chip, core):
        index = SLOT[chip] * 2 + core
        block, stats = expo.at[row_block(chip, core), :], stats_out.at[index]
        there = raw.at[:, pl.ds(pl.multiple_of(me * vocab, vocab), vocab)]
        if chip == own and core == 0:
            pltpu.make_async_copy(block, there, out_recv).start()
            pltpu.make_async_copy(stats, stats_in.at[me], st_recv).start()
        else:
            remote(stats, stats_in.at[me], st_send, st_recv, device(chip, core))
            remote(block, there, out_send, out_recv, device(chip, core))

    def deliver_all(chips):
        for core in (0, 1):
            for chip in chips:
                deliver(chip, core)

    def compute(chips, send_now=True):
        base = SLOT[chips[0]] * 2 * rows
        count = len(chips) * 2 * rows
        for chip in chips:
            for half in (0, 1):
                if chip == own and half:
                    continue
                ref = gathered.at[row_block(chip, 1), pl.ds(0, width) if chip == own else columns(half)]
                pltpu.make_async_copy(ref, ref, sib_recv.at[SLOT[chip] * 2 + half]).wait()

        def body(i, carry):
            at = pl.ds(pl.multiple_of(i * TILE, TILE), TILE)
            logits[0:count, at] = jnp.dot(
                gathered[base : base + count, :], weight[:, at], preferred_element_type=jnp.float32
            )
            return carry

        lax.fori_loop(0, vocab // TILE, body, 0)
        for core in (0, 1):
            for i, chip in enumerate(chips):
                part = i * 2 + core
                value = logits[part * rows : (part + 1) * rows, :]
                top = jnp.max(value, axis=1, keepdims=True)
                shift = value - top
                expf = jnp.exp(shift)
                total = jnp.sum(expf, axis=1, keepdims=True)
                tilt = jnp.sum(expf * shift, axis=1, keepdims=True)
                at = row_block(chip, core)
                expo[at, :] = expf.astype(jnp.bfloat16)
                packed = jnp.where(lane == 0, top, jnp.where(lane == 1, total, tilt))
                packed = jnp.concatenate([packed, jnp.zeros((128 - rows, 128), jnp.float32)], axis=0)
                index = SLOT[chip] * 2 + core
                turned = packed.T
                for k in range(3):
                    stats_out[index, :, k * 128 : (k + 1) * 128] = turned[k : k + 1, :]
                if send_now:
                    deliver(chip, core)

    stage_in(0).start()
    stage_in(1).start()
    scale_copy.wait()
    for block in range(vocab // BLOCK):
        dequantize(block)
        if block == 3:
            receive(0)
    receive(1)
    compute(STEPS[0], False)
    compute(STEPS[1], False)
    receive(2)
    compute(STEPS[2], False)
    receive(3)
    compute(STEPS[3])
    receive(4)
    compute(STEPS[4])
    receive(5)
    compute(STEPS[5])
    receive(6)
    receive(7)
    compute(STEPS[6])
    deliver_all([chip for pair in zip(STEPS[1], STEPS[2]) for chip in pair])
    receive(8)
    compute(STEPS[7])
    receive(9)
    deliver_all(STEPS[0])
    compute(STEPS[8])

    def wait_bytes(ref, sem):
        pltpu.make_async_copy(ref, ref, sem).wait()

    wait_bytes(gathered.at[pl.ds(0, 15 * rows), :], ici_send)
    wait_bytes(gathered.at[pl.ds(0, 16 * rows), :], sib_send)
    wait_bytes(expo.at[pl.ds(0, 31 * rows), :], out_send)
    wait_bytes(stats_out.at[pl.ds(0, 31)], st_send)
    wait_bytes(stats_in, st_recv)
    blocks = stats_in.shape[0]
    top, total, tilt = (stats_in[:, 0, k * 128 : (k + 1) * 128] for k in range(3))
    top_value = jnp.max(top, axis=0, keepdims=True)
    factor = jnp.exp(top - top_value)
    exp_sum = jnp.sum(total * factor, axis=0, keepdims=True)
    tilt_sum = jnp.sum(factor * (tilt + total * (top - top_value)), axis=0, keepdims=True)
    entropy[...] = jnp.log(exp_sum) - tilt_sum / exp_sum
    share_of_sum = jnp.concatenate([factor / exp_sum, jnp.zeros((128 - blocks, 128), jnp.float32)], axis=0)
    ratio[...] = share_of_sum.T[0:rows]
    wait_bytes(raw, out_recv)


def scale_kernel(rows, per_step, blocks, entropy_in, ratio, raw, out, entropy, ready, sems):
    vocab = raw.shape[1] // blocks
    entropy[...] = entropy_in[0, 0:rows]
    copies = []
    for step in range(blocks // per_step):
        cols = pl.ds(step * per_step * vocab, per_step * vocab)
        for b in range(step * per_step, (step + 1) * per_step):
            at = slice(b * vocab, (b + 1) * vocab)
            ready[:, at] = (raw[:, at].astype(jnp.float32) * ratio[:, b : b + 1]).astype(jnp.bfloat16)
        copies.append(pltpu.make_async_copy(ready.at[:, cols], out.at[:, cols], sems.at[step]))
        copies[-1].start()
    for copy in copies:
        copy.wait()


def shards(n_vocab, hidden, head_codes, head_scales):
    rows, width = hidden.shape
    vocab = head_codes.shape[0]
    hbm = pl.BlockSpec(memory_space=pltpu.HBM)
    vmem = pl.BlockSpec(memory_space=pltpu.VMEM)
    dma = pltpu.SemaphoreType.DMA
    raw, ratio, entropy = pl.pallas_call(
        functools.partial(head_kernel, rows),
        out_shape=(
            jax.ShapeDtypeStruct((rows, n_vocab * vocab), jnp.bfloat16),
            jax.ShapeDtypeStruct((rows, 128), jnp.float32),
            jax.ShapeDtypeStruct((1, 128), jnp.float32),
        ),
        in_specs=[hbm, hbm, hbm],
        out_specs=(vmem, vmem, vmem),
        scratch_shapes=[
            pltpu.SMEM(head_scales.shape, jnp.float32),
            pltpu.VMEM((n_vocab, 1, 384), jnp.float32),
            pltpu.VMEM((n_vocab * rows, width), jnp.bfloat16),
            pltpu.VMEM((width, vocab), jnp.bfloat16),
            pltpu.VMEM((2, BLOCK, width), jnp.bfloat16),
            pltpu.VMEM((4 * rows, vocab), jnp.float32),
            pltpu.VMEM((n_vocab * rows, vocab), jnp.bfloat16),
            pltpu.VMEM((n_vocab, 1, 384), jnp.float32),
            dma, dma, dma((2,)), dma, dma((len(LINKS) * ROUNDS,)), dma, dma((32,)), dma, dma, dma, dma,
        ],
        compiler_params=pltpu.CompilerParams(
            collective_id=0, has_side_effects=True, vmem_limit_bytes=50 << 20
        ),
        cost_estimate=pl.CostEstimate(
            flops=2 * n_vocab * rows * width * vocab,
            bytes_accessed=2 * vocab * width,
            transcendentals=n_vocab * rows * vocab,
        ),
        name="head",
    )(*(pltpu.with_memory_space_constraint(x, pltpu.HBM) for x in (hidden, head_codes, head_scales)))
    steps = 8
    probabilities, entropy = pl.pallas_call(
        functools.partial(scale_kernel, rows, n_vocab // steps, n_vocab),
        out_shape=(
            jax.ShapeDtypeStruct((rows, n_vocab * vocab), jnp.bfloat16),
            jax.ShapeDtypeStruct((rows,), jnp.float32),
        ),
        in_specs=[vmem, vmem, vmem],
        out_specs=(hbm, vmem),
        scratch_shapes=[pltpu.VMEM((rows, n_vocab * vocab), jnp.bfloat16), dma((steps,))],
        compiler_params=pltpu.CompilerParams(vmem_limit_bytes=16 << 20),
        name="scale",
    )(entropy, ratio, raw)
    return probabilities, entropy


def solution(mesh):
    placed = P(("batch", "vocab"), None)
    return jax.shard_map(
        functools.partial(shards, mesh.shape["vocab"]),
        mesh=mesh,
        in_specs=(placed, placed, placed),
        out_specs=(placed, P(("batch", "vocab"))),
        check_vma=False,
    )
```

```python
import functools

import jax
import jax.numpy as jnp
from jax import lax
from jax.experimental import pallas as pl
from jax.experimental.pallas import tpu as pltpu
from jax.sharding import PartitionSpec as P

MESH = pl.DeviceIdType.MESH
BLOCK = 128
TILE = 256

STEPS = [
    [(0, 0)], [(0, 1), (0, 3)], [(1, 0), (3, 0)], [(1, 3), (3, 1)], [(1, 1), (3, 3)],
    [(0, 2), (2, 0)], [(1, 2), (2, 1)], [(3, 2), (2, 3)], [(2, 2)],
]
SLOTS = [chip for chips in STEPS for chip in chips]
SLOT = {chip: slot for slot, chip in enumerate(SLOTS)}
def add(a, b):
    return ((a[0] + b[0]) % 4, (a[1] + b[1]) % 4)


def neg(a):
    return ((-a[0]) % 4, (-a[1]) % 4)


def link_sends(along_y, step):
    first, second = (0, 1) if along_y else (1, 0)
    quarter = 0 if step == 1 else 1

    def chip(other, this):
        return (other % 4, this % 4) if along_y else (this % 4, other % 4)

    return [
        (first, chip(0, 0), None),
        (second, chip(0, 0), None),
        (first, chip(0, -step), quarter),
        (second, chip(step, 0), None),
        (second, chip(-step, 0), None),
        (second, chip(0, -step), quarter),
        (second, chip(2, 0), None),
        (second, chip(1, -step), quarter),
        (second, chip(-1, -step), quarter),
        (second, chip(2, -step), quarter),
    ]


LINKS = [(move, link_sends(move[0] == 0, sum(move))) for move in ((0, 1), (0, -1), (1, 0), (-1, 0))]
ROUNDS = 10
AHEAD = 4


def send_turns():
    here = {}
    for move, sends in LINKS:
        for turn, (half, chip, _) in enumerate(sends):
            piece = (half, add(chip, neg(move)))
            here[piece] = max(turn, here.get(piece, 0))
    return [
        [max(here.get((half, chip), -1), turn - AHEAD if turn > 1 else -1) for turn, (half, chip, _) in enumerate(sends)]
        for _, sends in LINKS
    ]


SEND_TURNS = [[max(column) for column in zip(*send_turns(), (-1, -1, 0, 0, 1, 1, 2, 4, 4, 6))]] * len(LINKS)

def head_kernel(
    rows, hidden, codes, scales_in, raw, ratio, entropy,
    scales, stats_in, gathered, weight, staged, logits, expo, stats_out,
    scale_sem, copy_sem, stage_sem, ici_send, ici_recv, sib_send, sib_recv, out_send, out_recv, st_send, st_recv,
):
    width = hidden.shape[1]
    vocab = codes.shape[0]
    half_w, quarter_w = width // 2, width // 4
    me = lax.axis_index("vocab")
    z, y, c = me // 8, lax.rem(me // 2, 4), lax.rem(me, 2)

    def device(chip, core=0):
        index = (lax.rem(z + chip[0] % 4, 4) * 4 + lax.rem(y + chip[1] % 4, 4)) * 2 + lax.rem(c + core, 2)
        return {"vocab": index}

    def row_block(chip, core=0):
        return pl.ds(SLOT[chip] * 2 * rows + core * rows, rows)

    def columns(half, quarter=None):
        if quarter is None:
            return pl.ds(half * half_w, half_w)
        return pl.ds(half * half_w + quarter * quarter_w, quarter_w)

    def remote(src, dst, send, recv, target):
        pltpu.make_async_remote_copy(
            src_ref=src, dst_ref=dst, send_sem=send, recv_sem=recv, device_id=target, device_id_type=MESH
        ).start()

    def send(after):
        for turn in range(ROUNDS):
            for link, (move, sends) in enumerate(LINKS):
                if SEND_TURNS[link][turn] != after:
                    continue
                half, chip, quarter = sends[turn]
                cols = columns(half, quarter)
                src = gathered.at[row_block(chip), cols]
                dst = gathered.at[row_block(add(chip, neg(move))), cols]
                remote(src, dst, ici_send, ici_recv.at[link * ROUNDS + turn], device(move))

    def receive(turn):
        halves = []
        for link, (move, sends) in enumerate(LINKS):
            half, chip, quarter = sends[turn]
            chip = add(chip, neg(move))
            ref = gathered.at[row_block(chip), columns(half, quarter)]
            pltpu.make_async_copy(ref, ref, ici_recv.at[link * ROUNDS + turn]).wait()
            if (half, chip) not in halves:
                halves.append((half, chip))
        send(turn)
        for half, chip in halves:
            at = columns(half)
            remote(
                gathered.at[row_block(chip), at],
                gathered.at[row_block(chip, 1), at],
                sib_send,
                sib_recv.at[SLOT[chip] * 2 + half],
                device((0, 0), 1),
            )

    scale_copy = pltpu.make_async_copy(scales_in, scales, scale_sem)
    scale_copy.start()
    own = (0, 0)
    own_rows = gathered.at[row_block(own), :]
    own_copy = pltpu.make_async_copy(hidden, own_rows, copy_sem)
    own_copy.start()

    barrier = pltpu.get_barrier_semaphore()
    neighbours = [device(move) for move, _ in LINKS] + [device((0, 0), 1)]
    for neighbour in neighbours:
        pl.semaphore_signal(barrier, inc=1, device_id=neighbour, device_id_type=MESH)
    pl.semaphore_wait(barrier, len(neighbours))

    own_copy.wait()
    send(-1)
    remote(own_rows, gathered.at[row_block(own, 1), :], sib_send, sib_recv.at[0], device(own, 1))

    def stage_in(block):
        return pltpu.make_async_copy(
            codes.at[pl.ds(block * BLOCK, BLOCK), :], staged.at[block % 2], stage_sem.at[block % 2]
        )

    def dequantize(block):
        stage_in(block).wait()

        def body(i, carry):
            for j in range(4):
                d = i * 4 + j
                at = pl.ds(pl.multiple_of(d * BLOCK, BLOCK), BLOCK)
                tile = staged[block % 2, :, at].astype(jnp.float32) * scales[block, d]
                weight[at, pl.ds(block * BLOCK, BLOCK)] = tile.astype(jnp.bfloat16).T
            return carry

        lax.fori_loop(0, width // (4 * BLOCK), body, 0)
        if block + 2 < vocab // BLOCK:
            stage_in(block + 2).start()

    lane = lax.broadcasted_iota(jnp.int32, (rows, 128), 1)

    def deliver(chip, core):
        index = SLOT[chip] * 2 + core
        block, stats = expo.at[row_block(chip, core), :], stats_out.at[index]
        there = raw.at[:, pl.ds(pl.multiple_of(me * vocab, vocab), vocab)]
        if chip == own and core == 0:
            pltpu.make_async_copy(block, there, out_recv).start()
            pltpu.make_async_copy(stats, stats_in.at[me], st_recv).start()
        else:
            remote(stats, stats_in.at[me], st_send, st_recv, device(chip, core))
            remote(block, there, out_send, out_recv, device(chip, core))

    def deliver_all(chips):
        for core in (0, 1):
            for chip in chips:
                deliver(chip, core)

    def compute(chips, send_now=True):
        base = SLOT[chips[0]] * 2 * rows
        count = len(chips) * 2 * rows
        for chip in chips:
            for half in (0, 1):
                if chip == own and half:
                    continue
                ref = gathered.at[row_block(chip, 1), pl.ds(0, width) if chip == own else columns(half)]
                pltpu.make_async_copy(ref, ref, sib_recv.at[SLOT[chip] * 2 + half]).wait()

        def body(i, carry):
            at = pl.ds(pl.multiple_of(i * TILE, TILE), TILE)
            logits[0:count, at] = jnp.dot(
                gathered[base : base + count, :], weight[:, at], preferred_element_type=jnp.float32
            )
            return carry

        lax.fori_loop(0, vocab // TILE, body, 0)
        for core in (0, 1):
            for i, chip in enumerate(chips):
                part = i * 2 + core
                value = logits[part * rows : (part + 1) * rows, :]
                top = jnp.max(value, axis=1, keepdims=True)
                shift = value - top
                expf = jnp.exp(shift)
                total = jnp.sum(expf, axis=1, keepdims=True)
                tilt = jnp.sum(expf * shift, axis=1, keepdims=True)
                at = row_block(chip, core)
                expo[at, :] = expf.astype(jnp.bfloat16)
                packed = jnp.where(lane == 0, top, jnp.where(lane == 1, total, tilt))
                packed = jnp.concatenate([packed, jnp.zeros((128 - rows, 128), jnp.float32)], axis=0)
                index = SLOT[chip] * 2 + core
                turned = packed.T
                for k in range(3):
                    stats_out[index, :, k * 128 : (k + 1) * 128] = turned[k : k + 1, :]
                if send_now:
                    deliver(chip, core)

    stage_in(0).start()
    stage_in(1).start()
    scale_copy.wait()
    for block in range(vocab // BLOCK):
        dequantize(block)
        if block == 3:
            receive(0)
    receive(1)
    compute(STEPS[0], False)
    compute(STEPS[1], False)
    receive(2)
    compute(STEPS[2], False)
    receive(3)
    compute(STEPS[3])
    receive(4)
    compute(STEPS[4])
    receive(5)
    compute(STEPS[5], False)
    receive(6)
    deliver_all(STEPS[5])
    receive(7)
    compute(STEPS[6])
    deliver_all([chip for pair in zip(STEPS[1], STEPS[2]) for chip in pair])
    receive(8)
    compute(STEPS[7])
    receive(9)
    deliver_all(STEPS[0])
    compute(STEPS[8])

    def wait_bytes(ref, sem):
        pltpu.make_async_copy(ref, ref, sem).wait()

    wait_bytes(gathered.at[pl.ds(0, 15 * rows), :], ici_send)
    wait_bytes(gathered.at[pl.ds(0, 16 * rows), :], sib_send)
    wait_bytes(expo.at[pl.ds(0, 31 * rows), :], out_send)
    wait_bytes(stats_out.at[pl.ds(0, 31)], st_send)
    wait_bytes(stats_in, st_recv)
    blocks = stats_in.shape[0]
    top, total, tilt = (stats_in[:, 0, k * 128 : (k + 1) * 128] for k in range(3))
    top_value = jnp.max(top, axis=0, keepdims=True)
    factor = jnp.exp(top - top_value)
    exp_sum = jnp.sum(total * factor, axis=0, keepdims=True)
    tilt_sum = jnp.sum(factor * (tilt + total * (top - top_value)), axis=0, keepdims=True)
    entropy[...] = jnp.log(exp_sum) - tilt_sum / exp_sum
    share_of_sum = jnp.concatenate([factor / exp_sum, jnp.zeros((128 - blocks, 128), jnp.float32)], axis=0)
    ratio[...] = share_of_sum.T[0:rows]
    wait_bytes(raw, out_recv)


def scale_kernel(rows, per_step, blocks, entropy_in, ratio, raw, out, entropy, ready, sems):
    vocab = raw.shape[1] // blocks
    entropy[...] = entropy_in[0, 0:rows]
    copies = []
    for step in range(blocks // per_step):
        cols = pl.ds(step * per_step * vocab, per_step * vocab)
        for b in range(step * per_step, (step + 1) * per_step):
            at = slice(b * vocab, (b + 1) * vocab)
            ready[:, at] = (raw[:, at].astype(jnp.float32) * ratio[:, b : b + 1]).astype(jnp.bfloat16)
        copies.append(pltpu.make_async_copy(ready.at[:, cols], out.at[:, cols], sems.at[step]))
        copies[-1].start()
    for copy in copies:
        copy.wait()


def shards(n_vocab, hidden, head_codes, head_scales):
    rows, width = hidden.shape
    vocab = head_codes.shape[0]
    hbm = pl.BlockSpec(memory_space=pltpu.HBM)
    vmem = pl.BlockSpec(memory_space=pltpu.VMEM)
    dma = pltpu.SemaphoreType.DMA
    raw, ratio, entropy = pl.pallas_call(
        functools.partial(head_kernel, rows),
        out_shape=(
            jax.ShapeDtypeStruct((rows, n_vocab * vocab), jnp.bfloat16),
            jax.ShapeDtypeStruct((rows, 128), jnp.float32),
            jax.ShapeDtypeStruct((1, 128), jnp.float32),
        ),
        in_specs=[hbm, hbm, hbm],
        out_specs=(vmem, vmem, vmem),
        scratch_shapes=[
            pltpu.SMEM(head_scales.shape, jnp.float32),
            pltpu.VMEM((n_vocab, 1, 384), jnp.float32),
            pltpu.VMEM((n_vocab * rows, width), jnp.bfloat16),
            pltpu.VMEM((width, vocab), jnp.bfloat16),
            pltpu.VMEM((2, BLOCK, width), jnp.bfloat16),
            pltpu.VMEM((4 * rows, vocab), jnp.float32),
            pltpu.VMEM((n_vocab * rows, vocab), jnp.bfloat16),
            pltpu.VMEM((n_vocab, 1, 384), jnp.float32),
            dma, dma, dma((2,)), dma, dma((len(LINKS) * ROUNDS,)), dma, dma((32,)), dma, dma, dma, dma,
        ],
        compiler_params=pltpu.CompilerParams(
            collective_id=0, has_side_effects=True, vmem_limit_bytes=50 << 20
        ),
        cost_estimate=pl.CostEstimate(
            flops=2 * n_vocab * rows * width * vocab,
            bytes_accessed=2 * vocab * width,
            transcendentals=n_vocab * rows * vocab,
        ),
        name="head",
    )(*(pltpu.with_memory_space_constraint(x, pltpu.HBM) for x in (hidden, head_codes, head_scales)))
    steps = 8
    probabilities, entropy = pl.pallas_call(
        functools.partial(scale_kernel, rows, n_vocab // steps, n_vocab),
        out_shape=(
            jax.ShapeDtypeStruct((rows, n_vocab * vocab), jnp.bfloat16),
            jax.ShapeDtypeStruct((rows,), jnp.float32),
        ),
        in_specs=[vmem, vmem, vmem],
        out_specs=(hbm, vmem),
        scratch_shapes=[pltpu.VMEM((rows, n_vocab * vocab), jnp.bfloat16), dma((steps,))],
        compiler_params=pltpu.CompilerParams(vmem_limit_bytes=16 << 20),
        name="scale",
    )(entropy, ratio, raw)
    return probabilities, entropy


def solution(mesh):
    placed = P(("batch", "vocab"), None)
    return jax.shard_map(
        functools.partial(shards, mesh.shape["vocab"]),
        mesh=mesh,
        in_specs=(placed, placed, placed),
        out_specs=(placed, P(("batch", "vocab"))),
        check_vma=False,
    )
```
